128 devices in a mesh: row: 16 (over x, y), col: 8 (over z, core).
Axes of the slice: x: 4, y: 4, z: 4, core: 2. Of those that a mesh axis runs over, the one named last changes fastest.
Arguments:
- x_block: float32 [131072, 64], P(('col', 'row')), may hold values from -6 to 6
- r_block: float32 [131072, 64], P(('col', 'row')), may hold values from -6 to 6
- p_block: float32 [131072, 64], P(('col', 'row')), may hold values from -6 to 6
- neighbor_count: int32 [131072], P(('col', 'row')), may hold values from 8 to 32
- tile_values: bfloat16 [16, 8, 64, 128, 128], P('row', 'col'), may hold values from 0 to 0.079589844
- tile_row: int32 [16, 8, 64], P('row', 'col'), may hold values from 0 to 127
- tile_col: int32 [16, 8, 64], P('row', 'col'), may hold values from 0 to 63
- tile_count: int32 [16, 8], P('row', 'col'), may hold values from 16 to 64, as said below
Outputs:
- x_next: float32 [131072, 64], P(('col', 'row'))
- r_next: float32 [131072, 64], P(('col', 'row'))
- next_directions: float32 [131072, 64], P(('col', 'row'))
The draws below stay inside these ranges and needn't reach their ends.
Inputs may be any that keep to these rules, and one draw needn't show every extreme that they name: `tile_count`: slots at or past a device's count hold no tile; some device holds exactly 64 live tiles.
All inputs are finite; a program needn't handle non-finite values.
Results may differ from the reference program's by a relative error of at most 0.0055.
Values may be sent and summed in bfloat16 or wider, within the bound.
A program may use at most 128 MiB of HBM per device.

```python
import jax
import jax.numpy as jnp
from jax import lax

K = 64
TILE = 128
ITERS = 2
RR_STEPS = 3
RB = 8
TCAP = 64
NN = 131072
N_ROW = 16
N_COL = 8


def column_offsets(key):
    offset_key = jax.random.fold_in(key, 97)
    return jax.random.uniform(offset_key, (K,), jnp.float32, 1.2, 1.8)


def combine_parts(noise, offsets):
    return jnp.clip(noise + offsets[None, :], -6.0, 6.0).astype(jnp.float32)


def draw_x_block(key, part):
    offsets = column_offsets(key)
    key = jax.random.fold_in(key, 21)
    noise = jax.random.normal(key, (NN, K), jnp.float32)
    return combine_parts(noise, offsets)


def draw_r_block(key, part):
    offsets = column_offsets(key)
    key = jax.random.fold_in(key, 22)
    noise = jax.random.normal(key, (NN, K), jnp.float32)
    return combine_parts(noise, offsets)


def draw_p_block(key, part):
    offsets = column_offsets(key)
    key = jax.random.fold_in(key, 23)
    noise = jax.random.normal(key, (NN, K), jnp.float32)
    return combine_parts(noise, offsets)


def draw_tile_count(key, part):
    key = jax.random.fold_in(key, 11)
    count_key, pick_key = jax.random.split(key)
    counts = jax.random.randint(count_key, (N_ROW * N_COL,), TCAP // 4, TCAP + 1)
    chosen = jax.random.randint(pick_key, (), 0, N_ROW * N_COL)
    counts = jnp.where(jnp.arange(N_ROW * N_COL) == chosen, TCAP, counts)
    return counts.reshape(N_ROW, N_COL).astype(jnp.int32)


def touch_ends(entries, key, smallest, largest):
    longest = entries.shape.index(max(entries.shape))
    spots = []
    for shift in (0, 1):
        where = [jax.random.randint(jax.random.fold_in(key, axis), (), 0, length) for axis, length in enumerate(entries.shape)]
        where[longest] = (where[longest] + shift) % entries.shape[longest]
        spots.append(tuple(where))
    return entries.at[spots[0]].set(smallest).at[spots[1]].set(largest)


def shard_levels(key, dims, pieces, smallest, largest):
    gain, own = 1.0, jax.random.fold_in(key, 6)
    for axis_at, shards_of in pieces:
        steps = jnp.exp(jax.random.uniform(jax.random.fold_in(own, axis_at), (shards_of,), jnp.float32, smallest / len(pieces), largest / len(pieces)))
        gain = gain * jnp.repeat(steps, dims[axis_at] // shards_of).reshape([-1 if axis == axis_at else 1 for axis in range(len(dims))])
    return gain


def setup_inputs(seed: int = 0) -> dict:
    seeds = jax.random.split(jax.random.key(seed), 9)
    return {
        "x_block": draw_x_block(jax.random.fold_in(seeds[8], 71), 0),
        "r_block": draw_r_block(jax.random.fold_in(seeds[8], 71), 0),
        "p_block": draw_p_block(jax.random.fold_in(seeds[8], 71), 0),
        "neighbor_count": touch_ends(jax.random.randint(seeds[3], (NN,), 8, 33), jax.random.fold_in(seeds[3], 1), 8, 32).astype(jnp.int32),
        "tile_values": jnp.clip(0.079589844 * jax.random.uniform(seeds[4], (N_ROW, N_COL, TCAP, TILE, TILE), jnp.float32) ** shard_levels(seeds[4], (N_ROW, N_COL, TCAP, TILE, TILE), ((0, 16), (1, 8)), -0.2, 0.2), 0.0, 0.079589844).astype(jnp.bfloat16),
        "tile_row": touch_ends(jax.random.randint(seeds[5], (N_ROW, N_COL, TCAP), 0, N_ROW * RB), jax.random.fold_in(seeds[5], 1), 0, (N_ROW * RB) - 1).astype(jnp.int32),
        "tile_col": touch_ends(jax.random.randint(seeds[6], (N_ROW, N_COL, TCAP), 0, N_COL * RB), jax.random.fold_in(seeds[6], 1), 0, (N_COL * RB) - 1).astype(jnp.int32),
        "tile_count": draw_tile_count(jax.random.fold_in(seeds[8], 71), 0),
    }


def small_product(left, right):
    return jnp.matmul(left, right, precision=lax.Precision.HIGHEST)

def ritz_step(gram_g, gram_h, width_k):
    lower = jnp.linalg.cholesky(gram_g)
    half_left = lax.linalg.triangular_solve(lower, gram_h, left_side=True, lower=True)
    reduced = lax.linalg.triangular_solve(lower, half_left, left_side=False, lower=True, transpose_a=True)
    reduced = 0.5 * (reduced + reduced.T)
    order = reduced.shape[0]
    offset_operator = reduced + 4.0 * jnp.eye(order, dtype=jnp.float32)
    basis = jnp.eye(order, dtype=jnp.float32)[:, :width_k]
    for inner in range(RR_STEPS):
        basis = small_product(offset_operator, basis)
        factor = jnp.linalg.cholesky(small_product(basis.T, basis))
        basis = lax.linalg.triangular_solve(factor, basis, left_side=False, lower=True, transpose_a=True)
    theta = small_product(basis.T, small_product(reduced, basis))
    coeffs = lax.linalg.triangular_solve(lower, basis, left_side=True, lower=True, transpose_a=True)
    return (coeffs, theta)

def apply_affinity(scaled, tile_values, tile_row, tile_col, tile_count):
    panel_width = scaled.shape[1]
    block_total = NN // TILE
    block_list = scaled.reshape(block_total, TILE, panel_width)
    slot_ids = jnp.arange(TCAP, dtype=jnp.int32)

    def device_step(carry, device_id):
        row_index = device_id // N_COL
        col_index = device_id % N_COL
        tile_submatrix = tile_values[row_index, col_index]
        live_slot = slot_ids < tile_count[row_index, col_index]
        tile_submatrix = jnp.where(live_slot[:, None, None], tile_submatrix, jnp.zeros_like(tile_submatrix))
        target = (col_index * N_ROW * RB + tile_row[row_index, col_index]).astype(jnp.int32)
        local_col = tile_col[row_index, col_index]
        source = ((local_col // RB * N_ROW + row_index) * RB + local_col % RB).astype(jnp.int32)
        selected_entries = block_list[source]
        tile_contributions = jnp.einsum('iks,isq->ikq', tile_submatrix.astype(jnp.float32), selected_entries.astype(jnp.float32))
        return (carry.at[target].add(tile_contributions), None)
    start = jnp.zeros((block_total, TILE, panel_width), jnp.float32)
    device_ids = jnp.arange(N_ROW * N_COL, dtype=jnp.int32)
    result, unused = lax.scan(device_step, start, device_ids)
    return result.reshape(NN, panel_width)

def reference(x_block, r_block, p_block, neighbor_count, tile_values, tile_row, tile_col, tile_count):
    width_k = x_block.shape[1]
    degree_scale = (1.0 / jnp.sqrt(neighbor_count.astype(jnp.float32)))[:, None]
    basis_rows, resid_rows, search_rows = (x_block, r_block, p_block)
    for iteration in range(ITERS):
        block_panel = jnp.concatenate([basis_rows, resid_rows, search_rows], axis=1)
        scaled = (degree_scale * block_panel).astype(jnp.bfloat16)
        image = degree_scale * apply_affinity(scaled, tile_values, tile_row, tile_col, tile_count)
        gram_g = small_product(block_panel.T, block_panel) / NN
        cross = small_product(block_panel.T, image)
        gram_h = (cross + cross.T) / (2.0 * NN)
        coeffs, theta = ritz_step(gram_g, gram_h, width_k)
        search_coeffs = jnp.concatenate([jnp.zeros((width_k, width_k), jnp.float32), coeffs[width_k:]], axis=0)
        basis_rows = small_product(block_panel, coeffs)
        resid_rows = small_product(image, coeffs) - small_product(basis_rows, theta)
        search_rows = small_product(block_panel, search_coeffs)
    return (basis_rows, resid_rows, search_rows)
```

```python
import functools

import jax
import jax.numpy as jnp
from jax import lax
from jax.experimental import pallas as pl
from jax.experimental.pallas import tpu as pltpu
from jax.sharding import PartitionSpec as P

ITERS = 2
RR_STEPS = 3
K = 64
W3 = 3 * K
TILE = 128
BLOCKS = 8
SLOTS = 64
ROWS = 16
COLS = 8
SIDE = 4
NODES = BLOCKS * TILE
NODE_TOTAL = NODES * ROWS * COLS
F32 = jnp.float32
BF16 = jnp.bfloat16
MESH = pl.DeviceIdType.MESH
PIVOT_FLOOR = 1.0 / 64.0


def dot_nn(a, b):
    return lax.dot_general(
        a, b, (((1,), (0,)), ((), ())), precision=lax.Precision.HIGHEST, preferred_element_type=F32
    )


def dot_nt(a, b):
    return lax.dot_general(
        a, b, (((1,), (1,)), ((), ())), precision=lax.Precision.HIGHEST, preferred_element_type=F32
    )


def dot_tn(a, b):
    return lax.dot_general(
        a, b, (((0,), (0,)), ((), ())), precision=lax.Precision.HIGHEST, preferred_element_type=F32
    )


def eye(n):
    return jnp.where(
        lax.broadcasted_iota(jnp.int32, (n, n), 0) == lax.broadcasted_iota(jnp.int32, (n, n), 1), 1.0, 0.0
    ).astype(F32)


def inverse_factor(a):
    n = K
    both = jnp.concatenate([a, eye(n)], axis=1)
    tiles = [both[8 * t : 8 * t + 8, :] for t in range(n // 8)]
    sub = lax.broadcasted_iota(jnp.int32, (8, 2 * n), 0)
    for k in range(n):
        t0, kk = divmod(k, 8)
        row = tiles[t0][kk : kk + 1, :]
        scaled = row * (1.0 / row[:, k : k + 1])
        scaled = jnp.broadcast_to(scaled, (8, 2 * n))
        for t in range(t0, n // 8):
            col = jnp.broadcast_to(tiles[t][:, k : k + 1], (8, 2 * n))
            if t == t0:
                col = jnp.where(sub > kk, col, 0.0)
            tiles[t] = tiles[t] - col * scaled
    done = jnp.concatenate(tiles, axis=0)
    mask = eye(n)
    pivots = jnp.sum(done[:, :n] * mask, axis=1, keepdims=True)
    start = jnp.sum(a * mask, axis=1, keepdims=True)
    ratio = jnp.min(pivots / start)
    return done[:, n:] * lax.rsqrt(pivots), ratio


def main_kernel(first, width, center, *refs):
    vrows = width + 16 if center else width
    quarter = width // 4
    if first:
        x_ref, r_ref, p_ref, nc_ref, tiles_hbm, col_ref, link_ref = refs[:7]
        st_ref, ast_ref, h_ref, k_ref = refs[7:11]
        rest = refs[11:]
    else:
        st_ref, axp_ref, nc_ref, tiles_hbm, col_ref, link_ref = refs[:6]
        ast_ref, h_ref, k_ref = refs[6:9]
        rest = refs[9:]
    (
        tiles, vbuf, acc, sb, f1, n1, c1, tb, own, f2, n2, c2, part, ga, gb, gc, ha, hb, rsend, rrecv,
        load_sem, ag_s, ag_r, rs_s, rs_r, g_s, g_r, h_s, h_r, m_s, m_r,
    ) = rest

    row, col = lax.axis_index("row"), lax.axis_index("col")
    x, y = row // SIDE, lax.rem(row, SIDE)
    z, core = col // 2, lax.rem(col, 2)

    load = pltpu.make_async_copy(tiles_hbm, tiles, load_sem)
    load.start()

    barrier = pltpu.get_barrier_semaphore()
    for o in range(1, ROWS):
        pl.semaphore_signal(barrier, inc=1, device_id=(lax.rem(row + o, ROWS), col), device_id_type=MESH)
    for o in range(1, COLS):
        pl.semaphore_signal(barrier, inc=1, device_id=(row, lax.rem(col + o, COLS)), device_id_type=MESH)

    def remote(src, dst, ss, rs, where):
        return pltpu.make_async_remote_copy(
            src_ref=src, dst_ref=dst, send_sem=ss, recv_sem=rs, device_id=where, device_id_type=MESH
        )

    scale = 1.0 / jnp.sqrt(nc_ref[...].astype(F32))

    if first:
        for b in range(BLOCKS):
            at = pl.ds(b * TILE, TILE)
            st_ref[0:K, at] = jnp.transpose(x_ref[at, :])
            st_ref[K : 2 * K, at] = jnp.transpose(r_ref[at, :])
            st_ref[2 * K : W3, at] = jnp.transpose(p_ref[at, :])
    for b in range(BLOCKS):
        at = pl.ds(b * TILE, TILE)
        d_b = scale[b : b + 1, :]
        if first:
            vbuf[col, b, 0:width, :] = (st_ref[:, at] * d_b).astype(BF16)
        else:
            vbuf[col, b, 0:width, :] = (st_ref[K : 2 * K, at] * d_b).astype(BF16)
        if center:
            sub = lax.broadcasted_iota(jnp.int32, (16, TILE), 0)
            vbuf[col, b, width : width + 16, :] = jnp.where(sub == 0, d_b, 0.0).astype(BF16)

    pl.semaphore_wait(barrier, ROWS - 1 + COLS - 1)

    up = (row, lax.rem(z + 1, SIDE) * 2 + core)
    down = (row, lax.rem(z + 3, SIDE) * 2 + core)
    mate = (row, z * 2 + 1 - core)
    low, high = pl.ds(0, BLOCKS // 2), pl.ds(BLOCKS // 2, BLOCKS // 2)

    def gather(n, src, where):
        cp = remote(src, src, ag_s.at[n], ag_r.at[n], where)
        cp.start()
        return cp

    mine = vbuf.at[col]
    ag = {}
    ag[0] = gather(0, mine, up)
    ag[1] = gather(1, mine, down)
    ag[2] = gather(2, mine, mate)

    def pack(full):
        for c in range(W3 // 32):
            part[c] = full[32 * c : 32 * c + 32, 0:TILE]
        for c in range(2):
            part[6 + c] = jnp.zeros((32, TILE), F32)
            part[6 + c, :, 0:K] = full[2 * K + 32 * c : 2 * K + 32 * c + 32, TILE : TILE + K]

    def reduce_send(buf, ss, rs):
        buf[col] = part[col]
        cps = []
        for o in range(1, COLS):
            to = lax.rem(col + o, COLS)
            cp = remote(part.at[to], buf.at[col], ss.at[o - 1], rs.at[o - 1], (row, to))
            cp.start()
            cps.append(cp)
        return cps

    def reduce_cross(cps, buf, buf2, ss, rs):
        for cp in cps:
            cp.wait_recv()
        total = buf[0]
        for c in range(1, COLS):
            total = total + buf[c]
        buf2[row] = total
        cps2 = []
        for o in range(1, ROWS):
            to = lax.rem(row + o, ROWS)
            cp = remote(buf2.at[row], buf2.at[row], ss.at[6 + o], rs.at[6 + o], (to, col))
            cp.start()
            cps2.append(cp)
        return cps2

    def reduce_share(cps, buf2, out, ss, rs):
        for cp in cps:
            cp.wait_recv()
        total = buf2[0]
        for c in range(1, ROWS):
            total = total + buf2[c]
        out[col] = total
        cps2 = []
        for o in range(1, COLS):
            to = lax.rem(col + o, COLS)
            cp = remote(out.at[col], out.at[col], ss.at[21 + o], rs.at[21 + o], (row, to))
            cp.start()
            cps2.append(cp)
        return cps2

    stv = st_ref[...]
    pack(dot_nt(stv, stv))
    g1 = reduce_send(ga, g_s, g_r)

    ag[0].wait_recv()
    below = lax.rem(z + 3, SIDE) * 2 + core
    ag[3] = gather(3, vbuf.at[below, low], up)
    ag[4] = gather(4, vbuf.at[below], mate)
    ag[1].wait_recv()
    above = lax.rem(z + 1, SIDE) * 2 + core
    ag[5] = gather(5, vbuf.at[above, high], down)
    ag[6] = gather(6, vbuf.at[above], mate)

    g2 = reduce_cross(g1, ga, gb, g_s, g_r)

    across = lax.rem(z + 2, SIDE) * 2 + core
    ag[3].wait_recv()
    ag[7] = gather(7, vbuf.at[across, low], mate)
    ag[5].wait_recv()
    ag[8] = gather(8, vbuf.at[across, high], mate)

    g3 = reduce_share(g2, gb, gc, g_s, g_r)

    for n in (2, 4, 6, 7, 8):
        ag[n].wait_recv()
    load.wait()

    acc[SLOTS] = jnp.zeros((vrows, TILE), F32)

    def tile_step(t, carry):
        products = []
        for u in range(2):
            s = 2 * t + u
            c = col_ref[s]
            products.append(
                lax.dot_general(
                    vbuf[c // BLOCKS, lax.rem(c, BLOCKS)],
                    tiles[s],
                    (((1,), (1,)), ((), ())),
                    preferred_element_type=F32,
                )
            )
        for u in range(2):
            s = 2 * t + u
            acc[s] = products[u] + acc[link_ref[s]]
        return carry

    lax.fori_loop(0, SLOTS // 2, tile_step, 0)

    if center:
        ones = jnp.ones((TILE, TILE), BF16)
        total = jnp.zeros((vrows, TILE), F32)
        for j in range(COLS):
            for b in range(BLOCKS):
                total = total + lax.dot_general(
                    vbuf[j, b], ones, (((1,), (1,)), ((), ())), preferred_element_type=F32
                )
        mean = total[0:width, :] / total[width : width + 1, :]
        mean_row = jnp.transpose(mean[0:TILE, :])[0:1, :]
        mean_row2 = jnp.transpose(jnp.concatenate([mean[TILE:width, :], jnp.zeros((2 * TILE - width, TILE), F32)], axis=0))[0:1, :]

    def place_step(t, carry):
        dx, dy, b = t // (SIDE * BLOCKS), lax.rem(t // BLOCKS, SIDE), lax.rem(t, BLOCKS)
        block = acc[link_ref[SLOTS + t]]
        if center:
            rsend[dx * SIDE + dy, pl.ds(b, 1), :] = block[width : width + 1, :]
            block = block[0:width, :] - mean * block[width : width + 1, :]
        block = block.astype(BF16)
        for q in range(4):
            piece = block[q * quarter : (q + 1) * quarter, :]
            if q < 2:
                sb[q, dx, dy, b] = piece
            else:
                sb[q, dy, dx, b] = piece
        return carry

    lax.fori_loop(0, ROWS * BLOCKS, place_step, 0)

    def neighbour(axis, step):
        if axis == 0:
            return (lax.rem(x + step + SIDE, SIDE) * SIDE + y, col)
        return (x * SIDE + lax.rem(y + step + SIDE, SIDE), col)

    place = (x, y)

    def at(axis, step):
        return lax.rem(place[axis] + step + SIDE, SIDE)

    phases = []
    for q in range(4):
        axis, sign = q // 2, 1 - 2 * (q % 2)
        cp = remote(sb.at[q, at(axis, 2)], f1.at[q], rs_s.at[q], rs_r.at[q], neighbour(axis, sign))
        cp.start()
        phases.append([cp])
    for q in range(4):
        axis, sign = q // 2, 1 - 2 * (q % 2)
        cp = remote(sb.at[q, at(axis, -sign)], n1.at[q], rs_s.at[4 + q], rs_r.at[4 + q], neighbour(axis, -sign))
        cp.start()
        phases[q].append(cp)

    mcps = []
    if center:
        for i in range(ROWS):
            rsend[i, 8:9, :] = mean_row
            rsend[i, 9:10, :] = mean_row2
            rsend[i, 10:16, :] = jnp.zeros((6, TILE), F32)
        rrecv[row] = rsend[row]
        for o in range(1, ROWS):
            to = lax.rem(row + o, ROWS)
            cp = remote(rsend.at[to], rrecv.at[row], m_s.at[o - 1], m_r.at[o - 1], (to, col))
            cp.start()
            mcps.append(cp)

    for cp in g3:
        cp.wait_recv()

    def gram(r, c):
        if (r, c) == (2, 2):
            return jnp.concatenate([gc[6, :, 0:K], gc[7, :, 0:K]], axis=0) * (1.0 / NODE_TOTAL)
        return jnp.concatenate(
            [gc[2 * r, :, c * K : c * K + K], gc[2 * r + 1, :, c * K : c * K + K]], axis=0
        ) * (1.0 / NODE_TOTAL)

    k11, unused = inverse_factor(gram(0, 0))
    l21 = dot_nt(gram(1, 0), k11)
    s22 = gram(1, 1) - dot_nt(l21, l21)
    l31 = dot_nt(gram(2, 0), k11)
    k_ref[...] = jnp.zeros((W3, W3), F32)
    k_ref[0:K, 0:K] = k11

    for q in range(4):
        axis, sign = q // 2, 1 - 2 * (q % 2)
        phases[q][0].wait_recv()
        to = at(axis, sign)

        def meet(t, carry, q=q, to=to):
            d2, b = t // BLOCKS, lax.rem(t, BLOCKS)
            sb[q, to, d2, b] = (sb[q, to, d2, b].astype(F32) + f1[q, d2, b].astype(F32)).astype(BF16)
            return carry

        lax.fori_loop(0, SIDE * BLOCKS, meet, 0)
        cp = remote(sb.at[q, to], c1.at[q], rs_s.at[8 + q], rs_r.at[8 + q], neighbour(axis, sign))
        cp.start()
        phases[q].append(cp)

    k22, unused = inverse_factor(s22)
    k21 = -dot_nn(k22, dot_nn(l21, k11))
    l32 = dot_nt(gram(2, 1) - dot_nt(l31, l21), k22)
    s33 = gram(2, 2) - dot_nt(l31, l31) - dot_nt(l32, l32)
    k_ref[K : 2 * K, 0:K] = k21
    k_ref[K : 2 * K, K : 2 * K] = k22

    second = []
    for q in range(4):
        axis, sign = q // 2, 1 - 2 * (q % 2)
        phases[q][1].wait_recv()
        phases[q][2].wait_recv()
        me = place[axis]

        def merge(t, carry, q=q, me=me):
            d2, b = t // BLOCKS, lax.rem(t, BLOCKS)
            total = sb[q, me, d2, b].astype(F32) + n1[q, d2, b].astype(F32) + c1[q, d2, b].astype(F32)
            tb[q, d2, b] = total.astype(BF16)
            return carry

        lax.fori_loop(0, SIDE * BLOCKS, merge, 0)
        axis = 1 - axis
        cp = remote(tb.at[q, at(axis, 2)], f2.at[q], rs_s.at[12 + q], rs_r.at[12 + q], neighbour(axis, sign))
        cp.start()
        cp2 = remote(tb.at[q, at(axis, -sign)], n2.at[q], rs_s.at[16 + q], rs_r.at[16 + q], neighbour(axis, -sign))
        cp2.start()
        second.append([cp, cp2])
    for q in range(4):
        axis, sign = 1 - q // 2, 1 - 2 * (q % 2)
        second[q][0].wait_recv()
        to = at(axis, sign)

        def meet2(b, carry, q=q, to=to):
            tb[q, to, b] = (tb[q, to, b].astype(F32) + f2[q, b].astype(F32)).astype(BF16)
            return carry

        lax.fori_loop(0, BLOCKS, meet2, 0)
        cp = remote(tb.at[q, to], c2.at[q], rs_s.at[20 + q], rs_r.at[20 + q], neighbour(axis, sign))
        cp.start()
        second[q].append(cp)

    k33, unused = inverse_factor(s33)
    k32 = -dot_nn(k33, dot_nn(l32, k22))
    k31 = -dot_nn(k33, dot_nn(l31, k11) + dot_nn(l32, k21))
    k_ref[2 * K : W3, 0:K] = k31
    k_ref[2 * K : W3, K : 2 * K] = k32
    k_ref[2 * K : W3, 2 * K : W3] = k33

    if center:
        for cp in mcps:
            cp.wait_recv()
        means = jnp.concatenate([rrecv[:, 8, :], rrecv[:, 9, :]], axis=1)
        weights = jnp.concatenate([rrecv[:, b, :] for b in range(BLOCKS)], axis=1)
        back = dot_tn(means, weights)

    for q in range(4):
        me = place[1 - q // 2]
        second[q][1].wait_recv()
        second[q][2].wait_recv()
        for b in range(BLOCKS):
            total = tb[q, me, b].astype(F32) + n2[q, b].astype(F32) + c2[q, b].astype(F32)
            if center:
                total = total + back[q * quarter : (q + 1) * quarter, b * TILE : (b + 1) * TILE]
            total = total * scale[b : b + 1, :]
            base = q * quarter if first else K + q * quarter
            ast_ref[base : base + quarter, b * TILE : (b + 1) * TILE] = total
    if not first:
        ast_ref[0:K, :] = axp_ref[0:K, :]
        ast_ref[2 * K : W3, :] = axp_ref[K : 2 * K, :]

    for cp in g1:
        cp.wait_send()
    astv = ast_ref[...]
    pack(0.5 * (dot_nt(stv, astv) + dot_nt(astv, stv)))
    h1 = reduce_send(ha, h_s, h_r)
    h2 = reduce_cross(h1, ha, hb, h_s, h_r)
    h3 = reduce_share(h2, hb, h_ref, h_s, h_r)
    for cp in h3:
        cp.wait_recv()

    for n in range(9):
        ag[n].wait_send()
    for cps in phases + second + [mcps, g2, g3, h1, h2, h3]:
        for cp in cps:
            cp.wait_send()


def main_call(first, width, center, operands, collective_id):
    vrows = width + 16 if center else width
    quarter = width // 4
    vmem = pl.BlockSpec(memory_space=pltpu.VMEM)
    smem = pl.BlockSpec(memory_space=pltpu.SMEM)
    hbm = pl.BlockSpec(memory_space=pl.ANY)
    lead = [vmem] * (4 if first else 3)
    shapes = [
        jax.ShapeDtypeStruct((W3, NODES), F32),
        jax.ShapeDtypeStruct((COLS, 32, TILE), F32),
        jax.ShapeDtypeStruct((W3, W3), F32),
    ]
    if first:
        shapes = [jax.ShapeDtypeStruct((W3, NODES), F32)] + shapes
    dma = pltpu.SemaphoreType.DMA
    scratch = [
        pltpu.VMEM((SLOTS, TILE, TILE), BF16),
        pltpu.VMEM((COLS, BLOCKS, vrows, TILE), BF16),
        pltpu.VMEM((SLOTS + 1, vrows, TILE), F32),
        pltpu.VMEM((4, SIDE, SIDE, BLOCKS, quarter, TILE), BF16),
        pltpu.VMEM((4, SIDE, BLOCKS, quarter, TILE), BF16),
        pltpu.VMEM((4, SIDE, BLOCKS, quarter, TILE), BF16),
        pltpu.VMEM((4, SIDE, BLOCKS, quarter, TILE), BF16),
        pltpu.VMEM((4, SIDE, BLOCKS, quarter, TILE), BF16),
        pltpu.VMEM((8, TILE), F32),
        pltpu.VMEM((4, BLOCKS, quarter, TILE), BF16),
        pltpu.VMEM((4, BLOCKS, quarter, TILE), BF16),
        pltpu.VMEM((4, BLOCKS, quarter, TILE), BF16),
        pltpu.VMEM((COLS, 32, TILE), F32),
        pltpu.VMEM((COLS, 32, TILE), F32),
        pltpu.VMEM((ROWS, 32, TILE), F32),
        pltpu.VMEM((COLS, 32, TILE), F32),
        pltpu.VMEM((COLS, 32, TILE), F32),
        pltpu.VMEM((ROWS, 32, TILE), F32),
        pltpu.VMEM((ROWS, 16, TILE), F32),
        pltpu.VMEM((ROWS, 16, TILE), F32),
        dma(()),
        dma((9,)),
        dma((9,)),
        dma((24,)),
        dma((24,)),
        dma((29,)),
        dma((29,)),
        dma((29,)),
        dma((29,)),
        dma((15,)),
        dma((15,)),
    ]
    return pl.pallas_call(
        functools.partial(main_kernel, first, width, center),
        name="operator_first" if first else "operator_next",
        out_shape=shapes,
        in_specs=lead + [hbm, smem, smem] if first else [vmem, vmem, vmem, hbm, smem, smem],
        out_specs=[vmem] * len(shapes),
        scratch_shapes=scratch,
        compiler_params=pltpu.CompilerParams(
            collective_id=collective_id, has_side_effects=True, vmem_limit_bytes=56 << 20
        ),
    )(*operands)


def full_symmetric(h_ref):
    left = jnp.concatenate([h_ref[c] for c in range(6)], axis=0)
    corner = jnp.concatenate([h_ref[6, :, 0:K], h_ref[7, :, 0:K]], axis=0)
    right = jnp.concatenate([jnp.transpose(left[TILE:W3, :]), corner], axis=0)
    return jnp.concatenate([left, right], axis=1) * (1.0 / NODE_TOTAL)


def ritz_kernel(last, *refs):
    h_ref, k_ref, st_ref, ast_ref = refs[:4]
    basis_t = refs[-1]
    outs = refs[4:-1]
    kinv = k_ref[...]
    reduced = dot_nt(dot_nn(kinv, full_symmetric(h_ref)), kinv)
    reduced = 0.5 * (reduced + jnp.transpose(reduced))
    shifted = reduced + 4.0 * eye(W3)

    power = shifted[0:K, :]
    for inner in range(RR_STEPS - 1):
        power = dot_nn(power, shifted)
    factor, ratio = inverse_factor(dot_nt(power, power))
    basis_t[...] = dot_nn(factor, power)

    @pl.when(jnp.logical_not(ratio > PIVOT_FLOOR))
    def stepwise():
        basis_t[...] = eye(W3)[0:K, :]

        def step(t, carry):
            moved = dot_nn(basis_t[...], shifted)
            inverse, unused = inverse_factor(dot_nt(moved, moved))
            basis_t[...] = dot_nn(inverse, moved)
            return carry

        lax.fori_loop(0, RR_STEPS, step, 0)

    z_t = basis_t[...]
    theta = dot_nt(dot_nn(z_t, reduced), z_t)
    c_t = dot_nn(z_t, kinv)
    lane = lax.broadcasted_iota(jnp.int32, (K, W3), 1)
    cp_t = jnp.where(lane < K, 0.0, c_t)
    drop_t = dot_tn(theta, c_t)
    stv, astv = st_ref[...], ast_ref[...]
    left = dot_nn(jnp.concatenate([c_t, cp_t, drop_t], axis=0), stv)
    if last:
        resid = dot_nn(c_t, astv) - left[2 * K : W3, :]
        for b in range(BLOCKS):
            lanes = slice(b * TILE, (b + 1) * TILE)
            at = pl.ds(b * TILE, TILE)
            outs[0][at, :] = jnp.transpose(left[0:K, lanes])
            outs[1][at, :] = jnp.transpose(resid[:, lanes])
            outs[2][at, :] = jnp.transpose(left[K : 2 * K, lanes])
    else:
        image = dot_nn(jnp.concatenate([c_t, cp_t], axis=0), astv)
        outs[0][0:K, :] = left[0:K, :]
        outs[0][K : 2 * K, :] = image[0:K, :] - left[2 * K : W3, :]
        outs[0][2 * K : W3, :] = left[K : 2 * K, :]
        outs[1][...] = image


def ritz_call(last, h, kinv, st, ast):
    vmem = pl.BlockSpec(memory_space=pltpu.VMEM)
    if last:
        shapes = [jax.ShapeDtypeStruct((NODES, K), F32)] * 3
    else:
        shapes = [jax.ShapeDtypeStruct((W3, NODES), F32), jax.ShapeDtypeStruct((2 * K, NODES), F32)]
    return pl.pallas_call(
        functools.partial(ritz_kernel, last),
        name="ritz_last" if last else "ritz",
        out_shape=shapes,
        in_specs=[vmem] * 4,
        out_specs=[vmem] * len(shapes),
        scratch_shapes=[pltpu.VMEM((K, W3), F32)],
        compiler_params=pltpu.CompilerParams(vmem_limit_bytes=32 << 20),
    )(h, kinv, st, ast)


def per_device(
    x_block, r_block, p_block, neighbor_count, tile_values, tile_row, tile_col, tile_count
):
    tiles = tile_values[0, 0]
    targets = tile_row[0, 0]
    counts = neighbor_count.reshape(BLOCKS, TILE)
    slot = jnp.arange(SLOTS, dtype=jnp.int32)
    wanted = jnp.concatenate([targets, jnp.arange(ROWS * BLOCKS, dtype=jnp.int32)])
    before = jnp.concatenate([slot, jnp.full((ROWS * BLOCKS,), SLOTS, jnp.int32)])
    live = (slot < tile_count[0, 0])[None, :]
    found = (wanted[:, None] == targets[None, :]) & live & (slot[None, :] < before[:, None])
    link = jnp.max(jnp.where(found, slot[None, :], -1), axis=1)
    link = jnp.where(link < 0, SLOTS, link)
    st, ast, h, kinv = main_call(
        True, W3, True, (x_block, r_block, p_block, counts, tiles, tile_col[0, 0], link), 0
    )
    st, axp = ritz_call(False, h, kinv, st, ast)
    ast, h, kinv = main_call(False, K, False, (st, axp, counts, tiles, tile_col[0, 0], link), 1)
    return tuple(ritz_call(True, h, kinv, st, ast))


def solution(mesh):
    placed = (
        P(("col", "row"), None),
        P(("col", "row"), None),
        P(("col", "row"), None),
        P(("col", "row")),
        P("row", "col", None, None, None),
        P("row", "col", None),
        P("row", "col", None),
        P("row", "col"),
    )
    return jax.shard_map(
        per_device,
        mesh=mesh,
        in_specs=placed,
        out_specs=(P(("col", "row"), None), P(("col", "row"), None), P(("col", "row"), None)),
        check_vma=False,
    )
```

```python
import functools

import jax
import jax.numpy as jnp
from jax import lax
from jax.experimental import pallas as pl
from jax.experimental.pallas import tpu as pltpu
from jax.sharding import PartitionSpec as P

RR_STEPS = 3
K = 64
W3 = 3 * K
TILE = 128
BLOCKS = 8
SLOTS = 64
ROWS = 16
COLS = 8
SIDE = 4
NODES = BLOCKS * TILE
NODE_TOTAL = NODES * ROWS * COLS
F32 = jnp.float32
BF16 = jnp.bfloat16
MESH = pl.DeviceIdType.MESH
STEP = 8
HALF = BLOCKS // 2


def dot_nn(a, b):
    return lax.dot_general(
        a, b, (((1,), (0,)), ((), ())), precision=lax.Precision.HIGHEST, preferred_element_type=F32
    )


def dot_nt(a, b):
    return lax.dot_general(
        a, b, (((1,), (1,)), ((), ())), precision=lax.Precision.HIGHEST, preferred_element_type=F32
    )


def dot_tn(a, b):
    return lax.dot_general(
        a, b, (((0,), (0,)), ((), ())), precision=lax.Precision.HIGHEST, preferred_element_type=F32
    )


def eye(n):
    return jnp.where(
        lax.broadcasted_iota(jnp.int32, (n, n), 0) == lax.broadcasted_iota(jnp.int32, (n, n), 1), 1.0, 0.0
    ).astype(F32)


def inverse_factor(a):
    n = K
    both = jnp.concatenate([a, eye(n)], axis=1)
    tiles = [both[8 * t : 8 * t + 8, :] for t in range(n // 8)]
    shape = (8, 2 * n)
    sub = lax.broadcasted_iota(jnp.int32, shape, 0)
    done = []

    def lanes(v, k):
        return jnp.broadcast_to(v[:, k : k + 1], shape)

    for k in range(0, n, STEP):
        t0 = k // STEP
        r = [jnp.broadcast_to(tiles[t0][i : i + 1, :], shape) for i in range(STEP)]
        p = {(i, j): lanes(r[i], k + j) for i in range(STEP) for j in range(i, STEP)}
        pulled, gains = {}, {}
        row = None
        for i in range(0, STEP, 2):
            j = i + 1
            a_, b_, c_ = p[i, i], p[i, j], p[j, j]
            inverse = 1.0 / (a_ * c_ - b_ * b_)
            ia, ib, ic = a_ * inverse, b_ * inverse, c_ * inverse
            pulled[i], pulled[j] = ic * r[i] - ib * r[j], ia * r[j] - ib * r[i]
            for m in range(j + 1, STEP):
                gains[i, m] = ic * p[i, m] - ib * p[j, m]
                gains[j, m] = ia * p[j, m] - ib * p[i, m]
            for m in range(j + 1, STEP):
                r[m] = r[m] - (p[i, m] * pulled[i] + p[j, m] * pulled[j])
                for l in range(m, STEP):
                    p[m, l] = p[m, l] - (p[i, m] * gains[i, l] + p[j, m] * gains[j, l])
            slope = b_ / a_
            top = r[i] * lax.rsqrt(a_)
            low = (r[j] - slope * r[i]) * lax.rsqrt(c_ - slope * b_)
            row = top if row is None else jnp.where(sub == i, top, row)
            row = jnp.where(sub == j, low, row)
        done.append(row)
        for t in range(t0 + 1, n // 8):
            c = [lanes(tiles[t], k + j) for j in range(STEP)]
            change = None
            for i in range(0, STEP, 2):
                j = i + 1
                part = c[i] * pulled[i] + c[j] * pulled[j]
                change = part if change is None else change + part
                for m in range(j + 1, STEP):
                    c[m] = c[m] - (c[i] * gains[i, m] + c[j] * gains[j, m])
            tiles[t] = tiles[t] - change
    return jnp.concatenate(done, axis=0)[:, n:]


class Here:
    def __init__(self):
        self.row, self.col = lax.axis_index("row"), lax.axis_index("col")
        self.x, self.y = self.row // SIDE, lax.rem(self.row, SIDE)
        self.z, self.core = self.col // 2, lax.rem(self.col, 2)

    def at(self, axis, step):
        return lax.rem((self.x, self.y)[axis] + step + SIDE, SIDE)

    def beside(self, axis, step):
        if axis == 0:
            return (self.at(0, step) * SIDE + self.y, self.col)
        return (self.x * SIDE + self.at(1, step), self.col)

    def level(self, step):
        return lax.rem(self.z + step + SIDE, SIDE) * 2 + self.core

    def send(self, src, dst, send_sem, recv_sem, where):
        copy = pltpu.make_async_remote_copy(
            src_ref=src, dst_ref=dst, send_sem=send_sem, recv_sem=recv_sem, device_id=where, device_id_type=MESH
        )
        copy.start()
        return copy


def wait_for(ref, sem):
    pltpu.make_async_copy(ref, ref, sem).wait()


class Reduce:
    def __init__(self, here, part, spread, cross, out, sent, came):
        self.here, self.part, self.spread, self.cross, self.out = here, part, spread, cross, out
        self.sent, self.came = sent, came

    def pack(self, full):
        for c in range(W3 // 16):
            self.part[c] = full[16 * c : 16 * c + 16, 0:TILE]
        for c in range(K // 16):
            self.part[12 + c] = jnp.zeros((16, TILE), F32)
            self.part[12 + c, :, 0:K] = full[2 * K + 16 * c : 2 * K + 16 * c + 16, TILE : TILE + K]

    def start(self):
        h = self.here
        self.spread[h.row] = self.part[h.row]
        for o in range(1, ROWS):
            to = lax.rem(h.row + o, ROWS)
            h.send(self.part.at[to], self.spread.at[h.row], self.sent.at[0], self.came.at[0], (to, h.col))

    def over_col(self):
        h = self.here
        wait_for(self.spread.at[pl.ds(0, ROWS - 1)], self.came.at[0])
        total = self.spread[0]
        for c in range(1, ROWS):
            total = total + self.spread[c]
        self.cross[h.col] = total
        for o in range(1, COLS):
            to = lax.rem(h.col + o, COLS)
            h.send(self.cross.at[h.col], self.cross.at[h.col], self.sent.at[1], self.came.at[1], (h.row, to))

    def share(self):
        h = self.here
        wait_for(self.cross.at[pl.ds(0, COLS - 1)], self.came.at[1])
        total = self.cross[0]
        for c in range(1, COLS):
            total = total + self.cross[c]
        self.out[h.row] = total
        for o in range(1, ROWS):
            to = lax.rem(h.row + o, ROWS)
            h.send(self.out.at[h.row], self.out.at[h.row], self.sent.at[2], self.came.at[2], (to, h.col))

    def finish(self):
        wait_for(self.out.at[pl.ds(0, ROWS - 1)], self.came.at[2])

    def close(self):
        wait_for(self.part.at[pl.ds(0, ROWS - 1)], self.sent.at[0])
        wait_for(self.cross.at[pl.ds(0, COLS - 1)], self.sent.at[1])
        wait_for(self.out.at[pl.ds(0, ROWS - 1)], self.sent.at[2])


def symmetric(cross):
    return 0.5 * (cross + jnp.transpose(cross))


class Group:
    def __init__(self, here, width, extra, unroll, refs):
        self.here, self.width, self.extra, self.unroll = here, width, extra, unroll
        self.quarter = width // 4
        (
            self.v, self.acc, self.sb, self.f1, self.n1, self.c1, self.tb, self.last, self.sent, self.came
        ) = refs

    def prepare(self, st, base, scale):
        col = self.here.col
        for b in range(BLOCKS):
            d_b = scale[b : b + 1, :]
            block = st[base : base + self.width, b * TILE : (b + 1) * TILE] * d_b
            self.v[col, b, 0 : self.width, :] = block.astype(BF16)
            if self.extra:
                sub = lax.broadcasted_iota(jnp.int32, (16, TILE), 0)
                self.v[col, b, self.width : self.width + 16, :] = jnp.where(sub == 0, d_b, 0.0).astype(BF16)

    def pass_on(self, n, src, where):
        self.here.send(src, src, self.sent.at[0], self.came.at[n], where)

    def gather_start(self):
        h = self.here
        self.up, self.down = (h.row, h.level(1)), (h.row, h.level(-1))
        self.mate = (h.row, h.z * 2 + 1 - h.core)
        mine = self.v.at[h.col]
        self.pass_on(0, mine, self.up)
        self.pass_on(1, mine, self.down)
        self.pass_on(4, mine, self.mate)

    def gather_near(self):
        h = self.here
        wait_for(self.v.at[0], self.came.at[0])
        self.pass_on(2, self.v.at[h.level(-1), pl.ds(0, HALF)], self.up)
        self.pass_on(4, self.v.at[h.level(-1)], self.mate)
        wait_for(self.v.at[0], self.came.at[1])
        self.pass_on(3, self.v.at[h.level(1), pl.ds(HALF, HALF)], self.down)
        self.pass_on(4, self.v.at[h.level(1)], self.mate)

    def gather_far(self):
        h = self.here
        wait_for(self.v.at[0, pl.ds(0, HALF)], self.came.at[2])
        self.pass_on(4, self.v.at[h.level(2), pl.ds(0, HALF)], self.mate)
        wait_for(self.v.at[0, pl.ds(0, HALF)], self.came.at[3])
        self.pass_on(4, self.v.at[h.level(2), pl.ds(HALF, HALF)], self.mate)

    def gather_finish(self):
        wait_for(self.v.at[pl.ds(0, SIDE)], self.came.at[4])

    def near_total(self):
        h = self.here
        ones = jnp.ones((TILE, TILE), BF16)
        total = jnp.zeros((self.width + self.extra, TILE), F32)
        for j in (h.col, h.level(-1), h.level(1)):
            for b in range(BLOCKS):
                total = total + lax.dot_general(
                    self.v[j, b], ones, (((1,), (1,)), ((), ())), preferred_element_type=F32
                )
        return total

    def products(self, tiles, col_ref, link, start=0, stop=SLOTS):
        if start == 0:
            self.acc[SLOTS] = jnp.zeros((self.width + self.extra, TILE), F32)

        def step(t, carry):
            found = []
            for u in range(self.unroll):
                s = self.unroll * t + u
                c = col_ref[0, s]
                found.append(
                    lax.dot_general(
                        self.v[c // BLOCKS, lax.rem(c, BLOCKS)],
                        tiles[s],
                        (((1,), (1,)), ((), ())),
                        preferred_element_type=F32,
                    )
                )
            for u in range(self.unroll):
                s = self.unroll * t + u
                self.acc[s] = found[u] + self.acc[link[1, s]]
            return carry

        lax.fori_loop(start // self.unroll, stop // self.unroll, step, 0)

    def place(self, link, mean=None, weights=None):
        h, quarter = self.here, self.quarter

        def blocks_of(dx, dy):
            to = dx * SIDE + dy
            for b in range(BLOCKS):
                block = self.acc[link[0, to * BLOCKS + b]]
                if self.extra:
                    weight = block[self.width : self.width + 1, :]
                    weights[to, b : b + 1, :] = weight
                    block = block[0 : self.width, :]
                elif mean is not None:
                    weight = weights[to, b : b + 1, :]
                if mean is not None:
                    block = block - mean * weight
                block = block.astype(BF16)
                for q in range(4):
                    piece = block[q * quarter : (q + 1) * quarter, :]
                    if q < 2:
                        self.sb[q, dx, dy, b] = piece
                    else:
                        self.sb[q, dy, dx, b] = piece

        def far_x(t, carry):
            blocks_of(h.at(0, 2), t)
            return carry

        def far_y(t, carry):
            blocks_of(h.at(0, 3 + t), h.at(1, 2))
            return carry

        def others(t, carry):
            blocks_of(h.at(0, 3 + t // 3), h.at(1, 3 + lax.rem(t, 3)))
            return carry

        lax.fori_loop(0, SIDE, far_x, 0)
        self.far(0)
        lax.fori_loop(0, 3, far_y, 0)
        self.far(2)
        lax.fori_loop(0, 9, others, 0)
        self.near()

    def far(self, first):
        h = self.here
        for q in (first, first + 1):
            axis, sign = q // 2, 1 - 2 * (q % 2)
            h.send(self.sb.at[q, h.at(axis, 2)], self.f1.at[q], self.sent.at[1], self.came.at[5 + q], h.beside(axis, sign))

    def near(self):
        h = self.here
        for q in range(4):
            axis, sign = q // 2, 1 - 2 * (q % 2)
            h.send(self.sb.at[q, h.at(axis, -sign)], self.n1.at[q], self.sent.at[1], self.came.at[9 + q], h.beside(axis, -sign))

    def meet(self):
        h = self.here
        for q in range(4):
            axis, sign = q // 2, 1 - 2 * (q % 2)
            wait_for(self.f1.at[q], self.came.at[5 + q])
            to = h.at(axis, sign)

            def step(d, carry, q=q, to=to):
                total = self.sb[q, to, d].astype(F32) + self.f1[q, d].astype(F32)
                self.sb[q, to, d] = total.astype(BF16)
                return carry

            lax.fori_loop(0, SIDE, step, 0)
            h.send(self.sb.at[q, to], self.c1.at[q], self.sent.at[1], self.came.at[9 + q], h.beside(axis, sign))

    def turn(self):
        h = self.here
        for q in range(4):
            axis = q // 2
            wait_for(self.sb.at[q, pl.ds(0, 2)], self.came.at[9 + q])
            me = h.at(axis, 0)

            def step(d, carry, q=q, me=me):
                total = self.sb[q, me, d].astype(F32) + self.n1[q, d].astype(F32) + self.c1[q, d].astype(F32)
                self.tb[q, d] = total.astype(BF16)
                return carry

            lax.fori_loop(0, SIDE, step, 0)
            for o in (2, 1, 3):
                h.send(
                    self.tb.at[q, h.at(1 - axis, o)], self.last.at[q, o - 1], self.sent.at[2], self.came.at[13 + q],
                    h.beside(1 - axis, o),
                )

    def finish(self, out, base, scale, back=None):
        h, quarter = self.here, self.quarter
        for q in range(4):
            me = h.at(1 - q // 2, 0)
            wait_for(self.last.at[q], self.came.at[13 + q])
            first = base + q * quarter
            for b in range(BLOCKS):
                lanes = slice(b * TILE, (b + 1) * TILE)
                total = self.tb[q, me, b].astype(F32)
                for o in range(SIDE - 1):
                    total = total + self.last[q, o, b].astype(F32)
                if back is not None:
                    total = total + back[first : first + quarter, lanes]
                out[first : first + quarter, lanes] = total * scale[b : b + 1, :]

    def close(self):
        wait_for(self.v.at[pl.ds(0, COLS - 1)], self.sent.at[0])
        wait_for(self.sb.at[pl.ds(0, 3)], self.sent.at[1])
        wait_for(self.tb.at[pl.ds(0, 3)], self.sent.at[2])


class Factor:
    def __init__(self, sums, out):
        self.sums, self.out = sums, out

    def gram(self, r, c):
        if (r, c) == (2, 2):
            pieces = [self.sums[12 + i, :, 0:K] for i in range(4)]
        else:
            pieces = [self.sums[4 * r + i, :, c * K : c * K + K] for i in range(4)]
        return jnp.concatenate(pieces, axis=0) * (1.0 / NODE_TOTAL)

    def first(self):
        self.k11 = inverse_factor(self.gram(0, 0))
        self.l21 = dot_nt(self.gram(1, 0), self.k11)
        self.l31 = dot_nt(self.gram(2, 0), self.k11)
        self.s22 = self.gram(1, 1) - dot_nt(self.l21, self.l21)

    def second(self):
        self.k22 = inverse_factor(self.s22)
        self.l32 = dot_nt(self.gram(2, 1) - dot_nt(self.l31, self.l21), self.k22)
        self.s33 = self.gram(2, 2) - dot_nt(self.l31, self.l31) - dot_nt(self.l32, self.l32)

    def third(self):
        k33 = inverse_factor(self.s33)
        k21 = -dot_nn(self.k22, dot_nn(self.l21, self.k11))
        k32 = -dot_nn(k33, dot_nn(self.l32, self.k22))
        k31 = -dot_nn(k33, dot_nn(self.l31, self.k11) + dot_nn(self.l32, k21))
        self.out[...] = jnp.zeros((W3, W3), F32)
        for (r, c), block in {
            (0, 0): self.k11, (1, 0): k21, (1, 1): self.k22, (2, 0): k31, (2, 1): k32, (2, 2): k33
        }.items():
            self.out[r * K : r * K + K, c * K : c * K + K] = block


def full_symmetric(sums):
    left = jnp.concatenate([sums[c] for c in range(12)], axis=0)
    corner = jnp.concatenate([sums[12 + c, :, 0:K] for c in range(4)], axis=0)
    right = jnp.concatenate([jnp.transpose(left[TILE:W3, :]), corner], axis=0)
    return jnp.concatenate([left, right], axis=1) * (1.0 / NODE_TOTAL)


def ritz(sums, kinv):
    reduced = symmetric(dot_nt(dot_nn(kinv, full_symmetric(sums)), kinv))
    shifted = reduced + 4.0 * eye(W3)
    moved = shifted[0:K, :]
    for inner in range(RR_STEPS - 1):
        factor = inverse_factor(dot_nt(moved, moved))
        moved = dot_nn(factor, dot_nn(moved, shifted))
    factor = inverse_factor(dot_nt(moved, moved))
    theta = dot_nt(dot_nn(factor, dot_nt(dot_nn(moved, reduced), moved)), factor)
    c_t = dot_nn(factor, dot_nn(moved, kinv))
    return c_t, dot_tn(theta, c_t)


def whole_kernel(*refs):
    x_hbm, r_hbm, p_hbm, tiles_hbm = refs[:4]
    small_hbm = refs[4:8]
    h_out, kinv, st_out, ast_out = refs[8:12]
    st, ast, st2, ast2, tiles, link_v, link, weights, others = refs[12:21]
    nc_ref, row_ref, col_ref, count_ref = refs[21:25]
    load_sems, small_sems, link_sem, m_s, m_r = refs[25:30]
    rest = refs[30:]
    here = Here()
    reduces, groups = [], []
    for n in range(4):
        reduces.append(Reduce(here, *rest[:6]))
        rest = rest[6:]
    for width, extra, unroll in ((K, 16, 8), (2 * K, 0, 4), (K, 0, 8)):
        groups.append(Group(here, width, extra, unroll, rest[:10]))
        rest = rest[10:]
    sum_g, sum_h, sum_g2, sum_h2 = reduces
    thin, wide, again = groups
    row, col = here.row, here.col

    barrier = pltpu.get_barrier_semaphore()
    for o in range(1, ROWS):
        pl.semaphore_signal(barrier, inc=1, device_id=(lax.rem(row + o, ROWS), col), device_id_type=MESH)
    for o in range(1, COLS):
        pl.semaphore_signal(barrier, inc=1, device_id=(row, lax.rem(col + o, COLS)), device_id_type=MESH)
    loads = [
        pltpu.make_async_copy(p_hbm, st.at[pl.ds(2 * K, K)], load_sems.at[0]),
        pltpu.make_async_copy(x_hbm, st.at[pl.ds(0, K)], load_sems.at[1]),
        pltpu.make_async_copy(r_hbm, st.at[pl.ds(K, K)], load_sems.at[2]),
        pltpu.make_async_copy(tiles_hbm, tiles, load_sems.at[3]),
    ]
    small = [
        pltpu.make_async_copy(src, dst, small_sems.at[n])
        for n, (src, dst) in enumerate(zip(small_hbm, (nc_ref, row_ref, col_ref, count_ref)))
    ]
    for load in small + loads:
        load.start()
    for load in small:
        load.wait()

    along = lax.broadcasted_iota(jnp.int32, (SLOTS, SLOTS), 1)
    slot = lax.broadcasted_iota(jnp.int32, (SLOTS, SLOTS), 0)
    targets = jnp.broadcast_to(row_ref[...], (SLOTS, SLOTS))
    target = jnp.sum(jnp.where(slot == along, targets, 0), axis=1, keepdims=True)
    live = count_ref[0, 0]
    before = jnp.where((target == targets) & (slot < along) & (slot < live), slot, -1)
    before = jnp.max(before, axis=0, keepdims=True)
    slot = lax.broadcasted_iota(jnp.int32, (SLOTS, TILE), 0)
    final = jnp.where((target == lax.broadcasted_iota(jnp.int32, (SLOTS, TILE), 1)) & (slot < live), slot, -1)
    final = jnp.max(final, axis=0, keepdims=True)
    link_v[...] = jnp.full((8, TILE), SLOTS, jnp.int32)
    link_v[0:1, :] = jnp.where(final < 0, SLOTS, final)
    link_v[1:2, 0:SLOTS] = jnp.where(before < 0, SLOTS, before)
    link_copy = pltpu.make_async_copy(link_v, link, link_sem)
    link_copy.start()

    scale = 1.0 / jnp.sqrt(nc_ref[...].astype(F32))
    loads[0].wait()
    thin.prepare(st, 2 * K, scale)
    pl.semaphore_wait(barrier, ROWS - 1 + COLS - 1)

    thin.gather_start()
    loads[1].wait()
    loads[2].wait()
    wide.prepare(st, 0, scale)
    stv = st[...]
    sum_g.pack(dot_nt(stv, stv))
    sum_g.start()
    thin.gather_near()
    wide.gather_start()
    thin_total = thin.near_total()
    nodes = thin_total[K : K + 1, :]
    thin_mean = thin_total[0:K, :] / nodes
    sum_g.over_col()
    thin.gather_far()
    loads[3].wait()
    link_copy.wait()
    thin.gather_finish()
    thin.products(tiles, col_ref, link)
    wide.gather_near()
    thin.place(link, thin_mean, weights)
    wide.gather_far()
    sum_g.share()
    wide_mean = wide.near_total() / nodes
    weight_rows = [
        jnp.transpose(wide_mean)[0:1, :],
        jnp.transpose(jnp.concatenate([thin_mean, jnp.zeros((K, TILE), F32)], axis=0))[0:1, :],
    ]
    for i in range(ROWS):
        weights[i, 8:9, :] = weight_rows[0]
        weights[i, 9:10, :] = weight_rows[1]
        weights[i, 10:16, :] = jnp.zeros((6, TILE), F32)
    others[row] = weights[row]
    for o in range(1, ROWS):
        to = lax.rem(row + o, ROWS)
        here.send(weights.at[to], others.at[row], m_s, m_r, (to, col))
    wide.gather_finish()
    wide.products(tiles, col_ref, link, 0, SLOTS // 2)
    thin.meet()
    wide.products(tiles, col_ref, link, SLOTS // 2, SLOTS)
    wide.place(link, wide_mean, weights)
    sum_g.finish()
    factor = Factor(sum_g.out, kinv)
    factor.first()
    thin.turn()
    factor.second()
    wide.meet()
    factor.third()
    wait_for(others.at[pl.ds(0, ROWS - 1)], m_r)
    means = jnp.concatenate([others[:, 8, :], others[:, 9, :]], axis=1)
    back = dot_tn(means, jnp.concatenate([others[:, b, :] for b in range(BLOCKS)], axis=1))
    thin.finish(ast, 2 * K, scale, back)
    wide.turn()
    wide.finish(ast, 0, scale, back)
    astv = ast[...]
    sum_h.pack(symmetric(dot_nt(stv, astv)))
    sum_h.start()
    sum_h.over_col()
    sum_h.share()
    sum_h.finish()

    c_t, drop_t = ritz(sum_h.out, kinv[...])
    st2[K : 2 * K, :] = dot_nn(c_t, astv) - dot_nn(drop_t, stv)
    again.prepare(st2, K, scale)
    again.gather_start()
    cp_t = jnp.where(lax.broadcasted_iota(jnp.int32, (K, W3), 1) < K, 0.0, c_t)
    both = jnp.concatenate([c_t, cp_t], axis=0)
    moved = dot_nn(both, stv)
    st2[0:K, :] = moved[0:K, :]
    st2[2 * K : W3, :] = moved[K : 2 * K, :]
    stv2 = st2[...]
    sum_g2.pack(dot_nt(stv2, stv2))
    sum_g2.start()
    image = dot_nn(both, astv)
    ast2[0:K, :] = image[0:K, :]
    ast2[2 * K : W3, :] = image[K : 2 * K, :]
    again.gather_near()
    sum_g2.over_col()
    again.gather_far()
    again.gather_finish()
    again.products(tiles, col_ref, link)
    sum_g2.share()
    again.place(link)
    sum_g2.finish()
    again.meet()
    factor = Factor(sum_g2.out, kinv)
    factor.first()
    factor.second()
    again.turn()
    factor.third()
    again.finish(ast2, K, scale)
    astv2 = ast2[...]
    stores = [pltpu.make_async_copy(st2, st_out, load_sems.at[0]), pltpu.make_async_copy(ast2, ast_out, load_sems.at[1])]
    for store in stores:
        store.start()
    sum_h2.pack(symmetric(dot_nt(stv2, astv2)))
    sum_h2.start()
    sum_h2.over_col()
    sum_h2.share()
    sum_h2.finish()

    h_out[...] = sum_h2.out[...]
    for store in stores:
        store.wait()
    wait_for(weights.at[pl.ds(0, ROWS - 1)], m_s)
    for each in reduces + groups:
        each.close()


def whole_call(x_t, r_t, p_t, tiles, counts, tile_row, tile_col, tile_count):
    vmem = pl.BlockSpec(memory_space=pltpu.VMEM)
    hbm = pl.BlockSpec(memory_space=pltpu.HBM)
    dma = pltpu.SemaphoreType.DMA
    scratch = [
        pltpu.VMEM((W3, NODES), F32),
        pltpu.VMEM((W3, NODES), F32),
        pltpu.VMEM((W3, NODES), F32),
        pltpu.VMEM((W3, NODES), F32),
        pltpu.VMEM((SLOTS, TILE, TILE), BF16),
        pltpu.VMEM((8, TILE), jnp.int32),
        pltpu.SMEM((8, TILE), jnp.int32),
        pltpu.VMEM((ROWS, 16, TILE), F32),
        pltpu.VMEM((ROWS, 16, TILE), F32),
        pltpu.VMEM((BLOCKS, TILE), jnp.int32),
        pltpu.VMEM((1, SLOTS), jnp.int32),
        pltpu.SMEM((1, SLOTS), jnp.int32),
        pltpu.SMEM((1, 1), jnp.int32),
        dma((4,)),
        dma((4,)),
        dma(()),
        dma(()),
        dma(()),
    ]
    for n in range(4):
        scratch += [
            pltpu.VMEM((ROWS, 16, TILE), F32),
            pltpu.VMEM((ROWS, 16, TILE), F32),
            pltpu.VMEM((COLS, 16, TILE), F32),
            pltpu.VMEM((ROWS, 16, TILE), F32),
            dma((3,)),
            dma((3,)),
        ]
    for width, extra in ((K, 16), (2 * K, 0), (K, 0)):
        quarter = width // 4
        scratch += [
            pltpu.VMEM((COLS, BLOCKS, width + extra, TILE), BF16),
            pltpu.VMEM((SLOTS + 1, width + extra, TILE), F32),
            pltpu.VMEM((4, SIDE, SIDE, BLOCKS, quarter, TILE), BF16),
        ]
        scratch += [pltpu.VMEM((4, SIDE, BLOCKS, quarter, TILE), BF16)] * 4
        scratch += [pltpu.VMEM((4, SIDE - 1, BLOCKS, quarter, TILE), BF16)]
        scratch += [dma((3,)), dma((17,))]
    return pl.pallas_call(
        whole_kernel,
        name="iterations",
        out_shape=[
            jax.ShapeDtypeStruct((ROWS, 16, TILE), F32),
            jax.ShapeDtypeStruct((W3, W3), F32),
            jax.ShapeDtypeStruct((W3, NODES), F32),
            jax.ShapeDtypeStruct((W3, NODES), F32),
        ],
        in_specs=[hbm] * 8,
        out_specs=[vmem, vmem, hbm, hbm],
        scratch_shapes=scratch,
        compiler_params=pltpu.CompilerParams(
            collective_id=0, has_side_effects=True, vmem_limit_bytes=60 << 20
        ),
    )(x_t, r_t, p_t, tiles, counts, tile_row, tile_col, tile_count)


def last_kernel(sums, kinv, st_hbm, ast_hbm, x_out, r_out, p_out, st, ast, sems):
    loads = [pltpu.make_async_copy(st_hbm, st, sems.at[0]), pltpu.make_async_copy(ast_hbm, ast, sems.at[1])]
    for load in loads:
        load.start()
    c_t, drop_t = ritz(sums, kinv[...])
    for load in loads:
        load.wait()
    cp_t = jnp.where(lax.broadcasted_iota(jnp.int32, (K, W3), 1) < K, 0.0, c_t)
    moved = dot_nn(jnp.concatenate([c_t, cp_t, drop_t], axis=0), st[...])
    x_out[...] = moved[0:K, :]
    p_out[...] = moved[K : 2 * K, :]
    r_out[...] = dot_nn(c_t, ast[...]) - moved[2 * K : W3, :]


def last_call(sums, kinv, st, ast):
    vmem = pl.BlockSpec(memory_space=pltpu.VMEM)
    hbm = pl.BlockSpec(memory_space=pltpu.HBM)
    return pl.pallas_call(
        last_kernel,
        name="last_update",
        out_shape=[jax.ShapeDtypeStruct((K, NODES), F32)] * 3,
        in_specs=[vmem, vmem, hbm, hbm],
        out_specs=[vmem] * 3,
        scratch_shapes=[
            pltpu.VMEM((W3, NODES), F32), pltpu.VMEM((W3, NODES), F32), pltpu.SemaphoreType.DMA((2,))
        ],
        compiler_params=pltpu.CompilerParams(vmem_limit_bytes=60 << 20),
    )(sums, kinv, st, ast)


def per_device(
    x_block, r_block, p_block, neighbor_count, tile_values, tile_row, tile_col, tile_count
):
    whole = whole_call(
        x_block.T,
        r_block.T,
        p_block.T,
        tile_values[0, 0],
        neighbor_count.reshape(BLOCKS, TILE),
        tile_row[0],
        tile_col[0],
        tile_count,
    )

    x_t, r_t, p_t = last_call(*whole)
    return x_t.T, r_t.T, p_t.T


def solution(mesh):
    placed = (
        P(("col", "row"), None),
        P(("col", "row"), None),
        P(("col", "row"), None),
        P(("col", "row")),
        P("row", "col", None, None, None),
        P("row", "col", None),
        P("row", "col", None),
        P("row", "col"),
    )
    return jax.shard_map(
        per_device,
        mesh=mesh,
        in_specs=placed,
        out_specs=(P(("col", "row"), None), P(("col", "row"), None), P(("col", "row"), None)),
        check_vma=False,
    )
```

```python
import functools

import jax
import jax.numpy as jnp
from jax import lax
from jax.experimental import pallas as pl
from jax.experimental.pallas import tpu as pltpu
from jax.sharding import PartitionSpec as P

RR_STEPS = 3
K = 64
W3 = 3 * K
TILE = 128
BLOCKS = 8
SLOTS = 64
ROWS = 16
COLS = 8
SIDE = 4
NODES = BLOCKS * TILE
NODE_TOTAL = NODES * ROWS * COLS
F32 = jnp.float32
BF16 = jnp.bfloat16
MESH = pl.DeviceIdType.MESH
STEP = 8
HALF = BLOCKS // 2


def dot_nn(a, b):
    return lax.dot_general(
        a, b, (((1,), (0,)), ((), ())), precision=lax.Precision.HIGHEST, preferred_element_type=F32
    )


def dot_nt(a, b):
    return lax.dot_general(
        a, b, (((1,), (1,)), ((), ())), precision=lax.Precision.HIGHEST, preferred_element_type=F32
    )


def dot_tn(a, b):
    return lax.dot_general(
        a, b, (((0,), (0,)), ((), ())), precision=lax.Precision.HIGHEST, preferred_element_type=F32
    )


def eye(n):
    return jnp.where(
        lax.broadcasted_iota(jnp.int32, (n, n), 0) == lax.broadcasted_iota(jnp.int32, (n, n), 1), 1.0, 0.0
    ).astype(F32)


def inverse_factor(a):
    n = K
    both = jnp.concatenate([a, eye(n)], axis=1)
    tiles = [both[8 * t : 8 * t + 8, :] for t in range(n // 8)]
    shape = (8, 2 * n)
    sub = lax.broadcasted_iota(jnp.int32, shape, 0)
    done = []

    def lanes(v, k):
        return jnp.broadcast_to(v[:, k : k + 1], shape)

    for k in range(0, n, STEP):
        t0 = k // STEP
        r = [jnp.broadcast_to(tiles[t0][i : i + 1, :], shape) for i in range(STEP)]
        own = [lanes(tiles[t0], k + j) for j in range(STEP)]
        p = {(i, j): jnp.broadcast_to(own[j][i : i + 1, :], shape) for i in range(STEP) for j in range(i, STEP)}
        pulled, gains = {}, {}
        row = None
        for i in range(0, STEP, 2):
            j = i + 1
            a_, b_, c_ = p[i, i], p[i, j], p[j, j]
            inverse = 1.0 / (a_ * c_ - b_ * b_)
            ia, ib, ic = a_ * inverse, b_ * inverse, c_ * inverse
            pulled[i], pulled[j] = ic * r[i] - ib * r[j], ia * r[j] - ib * r[i]
            for m in range(j + 1, STEP):
                gains[i, m] = ic * p[i, m] - ib * p[j, m]
                gains[j, m] = ia * p[j, m] - ib * p[i, m]
            for m in range(j + 1, STEP):
                r[m] = r[m] - (p[i, m] * pulled[i] + p[j, m] * pulled[j])
                for l in range(m, STEP):
                    p[m, l] = p[m, l] - (p[i, m] * gains[i, l] + p[j, m] * gains[j, l])
            slope = b_ / a_
            top = r[i] * lax.rsqrt(a_)
            low = (r[j] - slope * r[i]) * lax.rsqrt(c_ - slope * b_)
            row = top if row is None else jnp.where(sub == i, top, row)
            row = jnp.where(sub == j, low, row)
        done.append(row)
        for t in range(t0 + 1, n // 8):
            c = [lanes(tiles[t], k + j) for j in range(STEP)]
            change = None
            for i in range(0, STEP, 2):
                j = i + 1
                part = c[i] * pulled[i] + c[j] * pulled[j]
                change = part if change is None else change + part
                for m in range(j + 1, STEP):
                    c[m] = c[m] - (c[i] * gains[i, m] + c[j] * gains[j, m])
            tiles[t] = tiles[t] - change
    return jnp.concatenate(done, axis=0)[:, n:]


class Here:
    def __init__(self):
        self.row, self.col = lax.axis_index("row"), lax.axis_index("col")
        self.x, self.y = self.row // SIDE, lax.rem(self.row, SIDE)
        self.z, self.core = self.col // 2, lax.rem(self.col, 2)

    def at(self, axis, step):
        return lax.rem((self.x, self.y)[axis] + step + SIDE, SIDE)

    def beside(self, axis, step):
        if axis == 0:
            return (self.at(0, step) * SIDE + self.y, self.col)
        return (self.x * SIDE + self.at(1, step), self.col)

    def level(self, step):
        return lax.rem(self.z + step + SIDE, SIDE) * 2 + self.core

    def send(self, src, dst, send_sem, recv_sem, where):
        copy = pltpu.make_async_remote_copy(
            src_ref=src, dst_ref=dst, send_sem=send_sem, recv_sem=recv_sem, device_id=where, device_id_type=MESH
        )
        copy.start()
        return copy


def wait_for(ref, sem):
    pltpu.make_async_copy(ref, ref, sem).wait()


class Reduce:
    def __init__(self, here, part, spread, cross, pair, out, sent, came):
        self.here, self.part, self.spread, self.cross, self.pair, self.out = here, part, spread, cross, pair, out
        self.sent, self.came = sent, came

    def pack(self, full):
        for c in range(W3 // 16):
            self.part[c] = full[16 * c : 16 * c + 16, 0:TILE]
        for c in range(K // 16):
            self.part[12 + c] = jnp.zeros((16, TILE), F32)
            self.part[12 + c, :, 0:K] = full[2 * K + 16 * c : 2 * K + 16 * c + 16, TILE : TILE + K]

    def start(self):
        h = self.here
        self.spread[h.row] = self.part[h.row]
        for o in range(1, ROWS):
            to = lax.rem(h.row + o, ROWS)
            h.send(self.part.at[to], self.spread.at[h.row], self.sent.at[0], self.came.at[0], (to, h.col))

    def over_z(self):
        h = self.here
        wait_for(self.spread.at[pl.ds(0, ROWS - 1)], self.came.at[0])
        total = self.spread[0]
        for c in range(1, ROWS):
            total = total + self.spread[c]
        self.cross[h.z] = total
        for o in range(1, SIDE):
            h.send(self.cross.at[h.z], self.cross.at[h.z], self.sent.at[1], self.came.at[1], (h.row, h.level(o)))

    def over_core(self):
        h = self.here
        wait_for(self.cross.at[pl.ds(0, SIDE - 1)], self.came.at[1])
        self.pair[h.core] = (self.cross[0] + self.cross[1]) + (self.cross[2] + self.cross[3])
        own = self.pair.at[h.core]
        h.send(own, own, self.sent.at[3], self.came.at[3], (h.row, h.z * 2 + 1 - h.core))

    def share(self):
        h = self.here
        wait_for(self.pair.at[0], self.came.at[3])
        self.out[h.row] = self.pair[0] + self.pair[1]
        for o in range(1, ROWS):
            to = lax.rem(h.row + o, ROWS)
            h.send(self.out.at[h.row], self.out.at[h.row], self.sent.at[2], self.came.at[2], (to, h.col))

    def finish(self):
        wait_for(self.out.at[pl.ds(0, ROWS - 1)], self.came.at[2])

    def close(self):
        wait_for(self.part.at[pl.ds(0, ROWS - 1)], self.sent.at[0])
        wait_for(self.cross.at[pl.ds(0, SIDE - 1)], self.sent.at[1])
        wait_for(self.pair.at[0], self.sent.at[3])
        wait_for(self.out.at[pl.ds(0, ROWS - 1)], self.sent.at[2])


def symmetric(cross):
    return 0.5 * (cross + jnp.transpose(cross))


class Group:
    def __init__(self, here, width, extra, unroll, refs):
        self.here, self.width, self.extra, self.unroll = here, width, extra, unroll
        self.quarter = width // 4
        (
            self.v, self.acc, self.sb, self.f1, self.n1, self.c1, self.tb, self.last, self.sent, self.came
        ) = refs

    def prepare(self, st, base, scale):
        col = self.here.col
        for b in range(BLOCKS):
            d_b = scale[b : b + 1, :]
            block = st[base : base + self.width, b * TILE : (b + 1) * TILE] * d_b
            self.v[col, b, 0 : self.width, :] = block.astype(BF16)
            if self.extra:
                sub = lax.broadcasted_iota(jnp.int32, (16, TILE), 0)
                self.v[col, b, self.width : self.width + 16, :] = jnp.where(sub == 0, d_b, 0.0).astype(BF16)

    def pass_on(self, n, src, where):
        self.here.send(src, src, self.sent.at[0], self.came.at[n], where)

    def gather_start(self):
        h = self.here
        self.up, self.down = (h.row, h.level(1)), (h.row, h.level(-1))
        self.mate = (h.row, h.z * 2 + 1 - h.core)
        mine = self.v.at[h.col]
        self.pass_on(0, mine, self.up)
        self.pass_on(1, mine, self.down)
        self.pass_on(4, mine, self.mate)

    def gather_start_straight(self):
        h = self.here
        self.mate = (h.row, h.z * 2 + 1 - h.core)
        mine = self.v.at[h.col]
        for n, o in enumerate((1, 3, 2)):
            self.pass_on(n, mine, (h.row, h.level(o)))
        self.pass_on(4, mine, self.mate)

    def gather_pass(self):
        h = self.here
        for n, o in enumerate((-1, -3, -2)):
            wait_for(self.v.at[0], self.came.at[n])
            self.pass_on(4, self.v.at[h.level(o)], self.mate)

    def gather_near(self):
        h = self.here
        wait_for(self.v.at[0], self.came.at[0])
        self.pass_on(2, self.v.at[h.level(-1), pl.ds(0, HALF)], self.up)
        self.pass_on(4, self.v.at[h.level(-1)], self.mate)
        wait_for(self.v.at[0], self.came.at[1])
        self.pass_on(3, self.v.at[h.level(1), pl.ds(HALF, HALF)], self.down)
        self.pass_on(4, self.v.at[h.level(1)], self.mate)

    def gather_far(self):
        h = self.here
        wait_for(self.v.at[0, pl.ds(0, HALF)], self.came.at[2])
        self.pass_on(4, self.v.at[h.level(2), pl.ds(0, HALF)], self.mate)
        wait_for(self.v.at[0, pl.ds(0, HALF)], self.came.at[3])
        self.pass_on(4, self.v.at[h.level(2), pl.ds(HALF, HALF)], self.mate)

    def gather_finish(self):
        wait_for(self.v.at[pl.ds(0, SIDE)], self.came.at[4])

    def near_total(self):
        h = self.here
        ones = jnp.ones((TILE, TILE), BF16)
        total = jnp.zeros((self.width + self.extra, TILE), F32)
        for j in (h.col, h.level(-1), h.level(1)):
            for b in range(BLOCKS):
                total = total + lax.dot_general(
                    self.v[j, b], ones, (((1,), (1,)), ((), ())), preferred_element_type=F32
                )
        return total

    def products(self, tiles, col_ref, link, start=0, stop=SLOTS):
        if start == 0:
            self.acc[SLOTS] = jnp.zeros((self.width + self.extra, TILE), F32)

        def step(t, carry):
            found = []
            for u in range(self.unroll):
                s = self.unroll * t + u
                c = col_ref[0, s]
                found.append(
                    lax.dot_general(
                        self.v[c // BLOCKS, lax.rem(c, BLOCKS)],
                        tiles[s],
                        (((1,), (1,)), ((), ())),
                        preferred_element_type=F32,
                    )
                )
            for u in range(self.unroll):
                s = self.unroll * t + u
                self.acc[s] = found[u] + self.acc[link[1, s]]
            return carry

        lax.fori_loop(start // self.unroll, stop // self.unroll, step, 0)

    def place(self, link, mean=None, weights=None):
        h, quarter = self.here, self.quarter

        def blocks_of(dx, dy):
            to = dx * SIDE + dy
            for b in range(BLOCKS):
                block = self.acc[link[0, to * BLOCKS + b]]
                if self.extra:
                    weight = block[self.width : self.width + 1, :]
                    weights[to, b : b + 1, :] = weight
                    block = block[0 : self.width, :]
                elif mean is not None:
                    weight = weights[to, b : b + 1, :]
                if mean is not None:
                    block = block - mean * weight
                block = block.astype(BF16)
                for q in range(4):
                    piece = block[q * quarter : (q + 1) * quarter, :]
                    if q < 2:
                        self.sb[q, dx, dy, b] = piece
                    else:
                        self.sb[q, dy, dx, b] = piece

        def far_x(t, carry):
            blocks_of(h.at(0, 2), t)
            return carry

        def far_y(t, carry):
            blocks_of(h.at(0, 3 + t), h.at(1, 2))
            return carry

        def others(t, carry):
            blocks_of(h.at(0, 3 + t // 3), h.at(1, 3 + lax.rem(t, 3)))
            return carry

        lax.fori_loop(0, SIDE, far_x, 0)
        self.far(0)
        lax.fori_loop(0, 3, far_y, 0)
        self.far(2)
        lax.fori_loop(0, 9, others, 0)

    def far(self, first):
        h = self.here
        for q in (first, first + 1):
            axis, sign = q // 2, 1 - 2 * (q % 2)
            h.send(self.sb.at[q, h.at(axis, 2)], self.f1.at[q], self.sent.at[1], self.came.at[5 + q], h.beside(axis, sign))

    def near(self):
        h = self.here
        for q in range(4):
            axis, sign = q // 2, 1 - 2 * (q % 2)
            h.send(self.sb.at[q, h.at(axis, -sign)], self.n1.at[q], self.sent.at[1], self.came.at[9 + q], h.beside(axis, -sign))

    def meet(self):
        h = self.here
        for q in range(4):
            axis, sign = q // 2, 1 - 2 * (q % 2)
            wait_for(self.f1.at[q], self.came.at[5 + q])
            to = h.at(axis, sign)

            def step(d, carry, q=q, to=to):
                total = self.sb[q, to, d].astype(F32) + self.f1[q, d].astype(F32)
                self.sb[q, to, d] = total.astype(BF16)
                return carry

            lax.fori_loop(0, SIDE, step, 0)
            h.send(self.sb.at[q, to], self.c1.at[q], self.sent.at[1], self.came.at[9 + q], h.beside(axis, sign))

    def turn(self):
        h = self.here
        for q in range(4):
            axis = q // 2
            wait_for(self.sb.at[q, pl.ds(0, 2)], self.came.at[9 + q])
            me = h.at(axis, 0)

            def step(d, carry, q=q, me=me):
                total = self.sb[q, me, d].astype(F32) + self.n1[q, d].astype(F32) + self.c1[q, d].astype(F32)
                self.tb[q, d] = total.astype(BF16)
                return carry

            lax.fori_loop(0, SIDE, step, 0)
            for o in (2, 1, 3):
                h.send(
                    self.tb.at[q, h.at(1 - axis, o)], self.last.at[q, o - 1], self.sent.at[2], self.came.at[13 + q],
                    h.beside(1 - axis, o),
                )

    def finish(self, out, base, scale, back=None):
        h, quarter = self.here, self.quarter
        for q in range(4):
            me = h.at(1 - q // 2, 0)
            wait_for(self.last.at[q], self.came.at[13 + q])
            first = base + q * quarter
            for b in range(BLOCKS):
                lanes = slice(b * TILE, (b + 1) * TILE)
                total = self.tb[q, me, b].astype(F32)
                for o in range(SIDE - 1):
                    total = total + self.last[q, o, b].astype(F32)
                if back is not None:
                    total = total + back[first : first + quarter, lanes]
                out[first : first + quarter, lanes] = total * scale[b : b + 1, :]

    def close(self):
        wait_for(self.v.at[pl.ds(0, COLS - 1)], self.sent.at[0])
        wait_for(self.sb.at[pl.ds(0, 3)], self.sent.at[1])
        wait_for(self.tb.at[pl.ds(0, 3)], self.sent.at[2])


class Factor:
    def __init__(self, sums, out):
        self.sums, self.out = sums, out

    def gram(self, r, c):
        if (r, c) == (2, 2):
            pieces = [self.sums[12 + i, :, 0:K] for i in range(4)]
        else:
            pieces = [self.sums[4 * r + i, :, c * K : c * K + K] for i in range(4)]
        return jnp.concatenate(pieces, axis=0) * (1.0 / NODE_TOTAL)

    def first(self):
        self.k11 = inverse_factor(self.gram(0, 0))
        self.l21 = dot_nt(self.gram(1, 0), self.k11)
        self.l31 = dot_nt(self.gram(2, 0), self.k11)
        self.s22 = self.gram(1, 1) - dot_nt(self.l21, self.l21)

    def second(self):
        self.k22 = inverse_factor(self.s22)
        self.l32 = dot_nt(self.gram(2, 1) - dot_nt(self.l31, self.l21), self.k22)
        self.s33 = self.gram(2, 2) - dot_nt(self.l31, self.l31) - dot_nt(self.l32, self.l32)

    def third(self):
        k33 = inverse_factor(self.s33)
        k21 = -dot_nn(self.k22, dot_nn(self.l21, self.k11))
        k32 = -dot_nn(k33, dot_nn(self.l32, self.k22))
        k31 = -dot_nn(k33, dot_nn(self.l31, self.k11) + dot_nn(self.l32, k21))
        self.out[...] = jnp.zeros((W3, W3), F32)
        for (r, c), block in {
            (0, 0): self.k11, (1, 0): k21, (1, 1): self.k22, (2, 0): k31, (2, 1): k32, (2, 2): k33
        }.items():
            self.out[r * K : r * K + K, c * K : c * K + K] = block


def full_symmetric(sums):
    left = jnp.concatenate([sums[c] for c in range(12)], axis=0)
    corner = jnp.concatenate([sums[12 + c, :, 0:K] for c in range(4)], axis=0)
    right = jnp.concatenate([jnp.transpose(left[TILE:W3, :]), corner], axis=0)
    return jnp.concatenate([left, right], axis=1) * (1.0 / NODE_TOTAL)


def ritz(sums, kinv):
    reduced = symmetric(dot_nt(dot_nn(kinv, full_symmetric(sums)), kinv))
    shifted = reduced + 4.0 * eye(W3)
    moved = shifted[0:K, :]
    for inner in range(RR_STEPS - 1):
        factor = inverse_factor(dot_nt(moved, moved))
        moved = dot_nn(factor, dot_nn(moved, shifted))
    factor = inverse_factor(dot_nt(moved, moved))
    theta = dot_nt(dot_nn(factor, dot_nt(dot_nn(moved, reduced), moved)), factor)
    c_t = dot_nn(factor, dot_nn(moved, kinv))
    return c_t, dot_tn(theta, c_t)


def whole_kernel(*refs):
    x_hbm, r_hbm, p_hbm, tiles_hbm = refs[:4]
    small_hbm = refs[4:8]
    h_out, kinv, st_out, ast_out = refs[8:12]
    st, ast, st2, ast2, tiles, link_v, link, weights, others = refs[12:21]
    nc_ref, row_ref, col_ref, count_ref = refs[21:25]
    load_sems, small_sems, link_sem, m_s, m_r = refs[25:30]
    rest = refs[30:]
    here = Here()
    reduces, groups = [], []
    for n in range(4):
        reduces.append(Reduce(here, *rest[:7]))
        rest = rest[7:]
    for width, extra, unroll in ((K, 16, 8), (K, 0, 8), (K, 0, 8), (K, 0, 8)):
        groups.append(Group(here, width, extra, unroll, rest[:10]))
        rest = rest[10:]
    sum_g, sum_h, sum_g2, sum_h2 = reduces
    of_p, of_r, of_x, again = groups
    row, col = here.row, here.col

    barrier = pltpu.get_barrier_semaphore()
    for o in range(1, ROWS):
        pl.semaphore_signal(barrier, inc=1, device_id=(lax.rem(row + o, ROWS), col), device_id_type=MESH)
    for o in range(1, COLS):
        pl.semaphore_signal(barrier, inc=1, device_id=(row, lax.rem(col + o, COLS)), device_id_type=MESH)
    loads = [
        pltpu.make_async_copy(p_hbm, st.at[pl.ds(2 * K, K)], load_sems.at[0]),
        pltpu.make_async_copy(x_hbm, st.at[pl.ds(0, K)], load_sems.at[1]),
        pltpu.make_async_copy(r_hbm, st.at[pl.ds(K, K)], load_sems.at[2]),
        pltpu.make_async_copy(tiles_hbm, tiles, load_sems.at[3]),
    ]
    small = [
        pltpu.make_async_copy(src, dst, small_sems.at[n])
        for n, (src, dst) in enumerate(zip(small_hbm, (nc_ref, row_ref, col_ref, count_ref)))
    ]
    for load in small + loads:
        load.start()
    for load in small:
        load.wait()

    along = lax.broadcasted_iota(jnp.int32, (SLOTS, SLOTS), 1)
    slot = lax.broadcasted_iota(jnp.int32, (SLOTS, SLOTS), 0)
    targets = jnp.broadcast_to(row_ref[...], (SLOTS, SLOTS))
    target = jnp.sum(jnp.where(slot == along, targets, 0), axis=1, keepdims=True)
    live = count_ref[0, 0]
    before = jnp.where((target == targets) & (slot < along) & (slot < live), slot, -1)
    before = jnp.max(before, axis=0, keepdims=True)
    slot = lax.broadcasted_iota(jnp.int32, (SLOTS, TILE), 0)
    final = jnp.where((target == lax.broadcasted_iota(jnp.int32, (SLOTS, TILE), 1)) & (slot < live), slot, -1)
    final = jnp.max(final, axis=0, keepdims=True)
    link_v[...] = jnp.full((8, TILE), SLOTS, jnp.int32)
    link_v[0:1, :] = jnp.where(final < 0, SLOTS, final)
    link_v[1:2, 0:SLOTS] = jnp.where(before < 0, SLOTS, before)
    link_copy = pltpu.make_async_copy(link_v, link, link_sem)
    link_copy.start()

    scale = 1.0 / jnp.sqrt(nc_ref[...].astype(F32))
    loads[0].wait()
    of_p.prepare(st, 2 * K, scale)
    pl.semaphore_wait(barrier, ROWS - 1 + COLS - 1)

    of_p.gather_start()
    loads[1].wait()
    loads[2].wait()
    of_r.prepare(st, K, scale)
    of_x.prepare(st, 0, scale)
    stv = st[...]
    sum_g.pack(dot_nt(stv, stv))
    sum_g.start()
    of_p.gather_near()
    of_r.gather_start()
    total = of_p.near_total()
    nodes = total[K : K + 1, :]
    mean_p = total[0:K, :] / nodes
    sum_g.over_z()
    of_p.gather_far()
    loads[3].wait()
    link_copy.wait()
    of_p.gather_finish()
    of_p.products(tiles, col_ref, link, 0, SLOTS // 2)
    of_r.gather_near()
    of_p.products(tiles, col_ref, link, SLOTS // 2, SLOTS)
    of_p.place(link, mean_p, weights)
    of_x.gather_start()
    sum_g.over_core()
    sum_g.share()
    of_r.gather_far()
    of_p.near()
    of_r.gather_finish()
    mean_r = of_r.near_total() / nodes
    of_r.products(tiles, col_ref, link)
    of_p.meet()
    of_r.place(link, mean_r, weights)
    of_x.gather_near()
    mean_x = of_x.near_total() / nodes
    of_x.gather_far()
    of_r.near()
    of_p.turn()
    of_x.gather_finish()
    of_x.products(tiles, col_ref, link)
    of_x.place(link, mean_x, weights)
    of_r.meet()
    weight_rows = [
        jnp.transpose(jnp.concatenate([mean_x, mean_r], axis=0))[0:1, :],
        jnp.transpose(jnp.concatenate([mean_p, jnp.zeros((K, TILE), F32)], axis=0))[0:1, :],
    ]
    for i in range(ROWS):
        weights[i, 8:9, :] = weight_rows[0]
        weights[i, 9:10, :] = weight_rows[1]
        weights[i, 10:16, :] = jnp.zeros((6, TILE), F32)
    others[row] = weights[row]
    for o in range(1, ROWS):
        to = lax.rem(row + o, ROWS)
        here.send(weights.at[to], others.at[row], m_s, m_r, (to, col))
    sum_g.finish()
    factor = Factor(sum_g.out, kinv)
    factor.first()
    of_x.near()
    of_x.meet()
    of_r.turn()
    factor.second()
    wait_for(others.at[pl.ds(0, ROWS - 1)], m_r)
    means = jnp.concatenate([others[:, 8, :], others[:, 9, :]], axis=1)
    back = dot_tn(means, jnp.concatenate([others[:, b, :] for b in range(BLOCKS)], axis=1))
    of_p.finish(ast, 2 * K, scale, back)
    of_x.turn()
    factor.third()
    of_r.finish(ast, K, scale, back)
    of_x.finish(ast, 0, scale, back)
    astv = ast[...]
    sum_h.pack(symmetric(dot_nt(stv, astv)))
    sum_h.start()
    sum_h.over_z()
    sum_h.over_core()
    sum_h.share()
    sum_h.finish()

    c_t, drop_t = ritz(sum_h.out, kinv[...])
    st2[K : 2 * K, :] = dot_nn(c_t, astv) - dot_nn(drop_t, stv)
    again.prepare(st2, K, scale)
    again.gather_start_straight()
    cp_t = jnp.where(lax.broadcasted_iota(jnp.int32, (K, W3), 1) < K, 0.0, c_t)
    both = jnp.concatenate([c_t, cp_t], axis=0)
    moved = dot_nn(both, stv)
    st2[0:K, :] = moved[0:K, :]
    st2[2 * K : W3, :] = moved[K : 2 * K, :]
    stv2 = st2[...]
    sum_g2.pack(dot_nt(stv2, stv2))
    sum_g2.start()
    sum_g2.over_z()
    again.gather_pass()
    again.gather_finish()
    again.products(tiles, col_ref, link)
    sum_g2.over_core()
    sum_g2.share()
    again.place(link)
    image = dot_nn(both, astv)
    ast2[0:K, :] = image[0:K, :]
    ast2[2 * K : W3, :] = image[K : 2 * K, :]
    again.near()
    again.meet()
    sum_g2.finish()
    factor = Factor(sum_g2.out, kinv)
    factor.first()
    factor.second()
    again.turn()
    factor.third()
    again.finish(ast2, K, scale)
    astv2 = ast2[...]
    stores = [pltpu.make_async_copy(st2, st_out, load_sems.at[0]), pltpu.make_async_copy(ast2, ast_out, load_sems.at[1])]
    for store in stores:
        store.start()
    sum_h2.pack(symmetric(dot_nt(stv2, astv2)))
    sum_h2.start()
    sum_h2.over_z()
    sum_h2.over_core()
    sum_h2.share()
    sum_h2.finish()

    h_out[...] = sum_h2.out[...]
    for store in stores:
        store.wait()
    wait_for(weights.at[pl.ds(0, ROWS - 1)], m_s)
    for each in reduces + groups:
        each.close()


def whole_call(x_t, r_t, p_t, tiles, counts, tile_row, tile_col, tile_count):
    vmem = pl.BlockSpec(memory_space=pltpu.VMEM)
    hbm = pl.BlockSpec(memory_space=pltpu.HBM)
    dma = pltpu.SemaphoreType.DMA
    scratch = [
        pltpu.VMEM((W3, NODES), F32),
        pltpu.VMEM((W3, NODES), F32),
        pltpu.VMEM((W3, NODES), F32),
        pltpu.VMEM((W3, NODES), F32),
        pltpu.VMEM((SLOTS, TILE, TILE), BF16),
        pltpu.VMEM((8, TILE), jnp.int32),
        pltpu.SMEM((8, TILE), jnp.int32),
        pltpu.VMEM((ROWS, 16, TILE), F32),
        pltpu.VMEM((ROWS, 16, TILE), F32),
        pltpu.VMEM((BLOCKS, TILE), jnp.int32),
        pltpu.VMEM((1, SLOTS), jnp.int32),
        pltpu.SMEM((1, SLOTS), jnp.int32),
        pltpu.SMEM((1, 1), jnp.int32),
        dma((4,)),
        dma((4,)),
        dma(()),
        dma(()),
        dma(()),
    ]
    for n in range(4):
        scratch += [
            pltpu.VMEM((ROWS, 16, TILE), F32),
            pltpu.VMEM((ROWS, 16, TILE), F32),
            pltpu.VMEM((SIDE, 16, TILE), F32),
            pltpu.VMEM((2, 16, TILE), F32),
            pltpu.VMEM((ROWS, 16, TILE), F32),
            dma((4,)),
            dma((4,)),
        ]
    for width, extra in ((K, 16), (K, 0), (K, 0), (K, 0)):
        quarter = width // 4
        scratch += [
            pltpu.VMEM((COLS, BLOCKS, width + extra, TILE), BF16),
            pltpu.VMEM((SLOTS + 1, width + extra, TILE), F32),
            pltpu.VMEM((4, SIDE, SIDE, BLOCKS, quarter, TILE), BF16),
        ]
        scratch += [pltpu.VMEM((4, SIDE, BLOCKS, quarter, TILE), BF16)] * 4
        scratch += [pltpu.VMEM((4, SIDE - 1, BLOCKS, quarter, TILE), BF16)]
        scratch += [dma((3,)), dma((17,))]
    return pl.pallas_call(
        whole_kernel,
        name="iterations",
        out_shape=[
            jax.ShapeDtypeStruct((ROWS, 16, TILE), F32),
            jax.ShapeDtypeStruct((W3, W3), F32),
            jax.ShapeDtypeStruct((W3, NODES), F32),
            jax.ShapeDtypeStruct((W3, NODES), F32),
        ],
        in_specs=[hbm] * 8,
        out_specs=[vmem, vmem, hbm, hbm],
        scratch_shapes=scratch,
        compiler_params=pltpu.CompilerParams(
            collective_id=0, has_side_effects=True, vmem_limit_bytes=60 << 20
        ),
    )(x_t, r_t, p_t, tiles, counts, tile_row, tile_col, tile_count)


def last_kernel(sums, kinv, st_hbm, ast_hbm, x_out, r_out, p_out, st, ast, sems):
    loads = [pltpu.make_async_copy(st_hbm, st, sems.at[0]), pltpu.make_async_copy(ast_hbm, ast, sems.at[1])]
    for load in loads:
        load.start()
    c_t, drop_t = ritz(sums, kinv[...])
    for load in loads:
        load.wait()
    cp_t = jnp.where(lax.broadcasted_iota(jnp.int32, (K, W3), 1) < K, 0.0, c_t)
    moved = dot_nn(jnp.concatenate([c_t, cp_t, drop_t], axis=0), st[...])
    x_out[...] = moved[0:K, :]
    p_out[...] = moved[K : 2 * K, :]
    r_out[...] = dot_nn(c_t, ast[...]) - moved[2 * K : W3, :]


def last_call(sums, kinv, st, ast):
    vmem = pl.BlockSpec(memory_space=pltpu.VMEM)
    hbm = pl.BlockSpec(memory_space=pltpu.HBM)
    return pl.pallas_call(
        last_kernel,
        name="last_update",
        out_shape=[jax.ShapeDtypeStruct((K, NODES), F32)] * 3,
        in_specs=[vmem, vmem, hbm, hbm],
        out_specs=[vmem] * 3,
        scratch_shapes=[
            pltpu.VMEM((W3, NODES), F32), pltpu.VMEM((W3, NODES), F32), pltpu.SemaphoreType.DMA((2,))
        ],
        compiler_params=pltpu.CompilerParams(vmem_limit_bytes=60 << 20),
    )(sums, kinv, st, ast)


def per_device(
    x_block, r_block, p_block, neighbor_count, tile_values, tile_row, tile_col, tile_count
):
    whole = whole_call(
        x_block.T,
        r_block.T,
        p_block.T,
        tile_values[0, 0],
        neighbor_count.reshape(BLOCKS, TILE),
        tile_row[0],
        tile_col[0],
        tile_count,
    )

    x_t, r_t, p_t = last_call(*whole)
    return x_t.T, r_t.T, p_t.T


def solution(mesh):
    placed = (
        P(("col", "row"), None),
        P(("col", "row"), None),
        P(("col", "row"), None),
        P(("col", "row")),
        P("row", "col", None, None, None),
        P("row", "col", None),
        P("row", "col", None),
        P("row", "col"),
    )
    return jax.shard_map(
        per_device,
        mesh=mesh,
        in_specs=placed,
        out_specs=(P(("col", "row"), None), P(("col", "row"), None), P(("col", "row"), None)),
        check_vma=False,
    )
```
